32 devices in a mesh: uv: 16 (over z, x, core), wa: 2 (over y).
Axes of the slice: x: 2, y: 2, z: 4, core: 2. Of those that a mesh axis runs over, the one named last changes fastest.
Arguments:
- visibilities: bfloat16 [2048, 2, 256], P(('uv', 'wa')), may hold values from -6 to 6
- positions: bfloat16 [2048, 2, 256], P(('uv', 'wa')), may hold values from 0 to 1
- tile_scale: bfloat16 [2048], P(('uv', 'wa')), may hold values from 0.29882812 to 3
- owner: int32 [2048, 1], P(('uv', 'wa')), may hold values from 0 to 15; in each aligned block of 64 rows (0 to 63, 64 to 127, ...) at most 6 rows name the same one
- block_id: int32 [2048], P(('uv', 'wa')), may hold values from 0 to 255
- w_slot: int32 [2048], P(('uv', 'wa')), may hold values from 0 to 1
- screen: bfloat16 [4, 256, 32768], P('wa', 'uv'), may hold values from -3.140625 to 3.140625
Outputs:
- merged: float32 [2, 256, 32768], P(None, 'uv', 'wa')
The draws below stay inside these ranges and needn't reach their ends.
Inputs may be any that keep to these rules, and one draw needn't show every extreme that they name: Among the 64 tiles of one device no owner is named by more than 6 tiles, a bound that some block reaches.
All inputs are finite; a program needn't handle non-finite values.
Results may differ from the reference program's by a relative error of at most 0.0035.
Values may be sent and summed in bfloat16 or wider, within the bound.
A program may use at most 64 MiB of HBM per device.

```python
import math
import jax
import jax.numpy as jnp
import numpy as np
from jax import lax

TILE = 256
KR = 16
KC = 128
BLK_R = 1
BLK_C = 256
LAY_DEV = 2
TD = 64
NBLK = 256
WC = 32768
ROWS = 256
LAYERS = 4
CAP = 6
TILES = 2048
N_UV = 16
N_WA = 2


def plant(result, stream_key, least, top_value):
    place = [jax.random.randint(jax.random.fold_in(stream_key, axis), (), 0, length) for axis, length in enumerate(result.shape)]
    widest = result.shape.index(max(result.shape))
    next_to = place[:widest] + [(place[widest] + 1) % result.shape[widest]] + place[widest + 1:]
    return result.at[tuple(place)].set(least).at[tuple(next_to)].set(top_value)


def steps_of(own_key, extent, cuts, least, high):
    def one(dim, blocks):
        steps = jax.random.uniform(jax.random.fold_in(jax.random.fold_in(own_key, 6), dim), (blocks,), jnp.float32, least / len(cuts), high / len(cuts))
        return jnp.repeat(jnp.exp(steps), extent[dim] // blocks).reshape((-1,) + (1,) * (len(extent) - dim - 1))

    gain = one(*cuts[0])
    for cut in cuts[1:]:
        gain = gain * one(*cut)
    return gain


def shared_out(key, own, number, rows, amount, top, limit, slope):
    sequence = jax.random.permutation(key, amount)
    heavy_load, common = portions_of(amount, rows * top, limit, slope, True), portions_of(amount, rows * top, limit, slope, False)
    places = jnp.arange(amount)

    def named(sizes, turn):
        used = int((sizes > 0).sum())
        fixed = max(1, used // 4)
        shifted = fixed + (places - fixed + turn * (used - fixed)) % max(1, amount - fixed)
        return jnp.zeros((amount,), jnp.int32).at[sequence[jnp.where(places < fixed, places, shifted)]].set(jnp.asarray(sizes, jnp.int32))

    sizes = jnp.where(number % 4 == 0, named(heavy_load, number // 4), named(common, number - number // 4 - 1))
    mixed = jax.random.permutation(jax.random.fold_in(own, 3), amount)
    giver, receiver = mixed[0:amount // 2 * 2:2], mixed[1:amount // 2 * 2:2]
    slack = jnp.minimum(sizes[giver] - 1, limit - sizes[receiver]) // 2
    slack = jnp.where((giver == sequence[0]) | (receiver == sequence[0]) | (sizes[receiver] == 0), 0, jnp.maximum(slack, 0))
    shifted = jax.random.randint(jax.random.fold_in(own, 4), (amount // 2,), 0, 1 << 20) % (slack + 1)
    sizes = sizes.at[giver].add(-shifted).at[receiver].add(shifted)
    items = jnp.searchsorted(jnp.cumsum(sizes), jnp.arange(rows * top), side="right").astype(jnp.int32)
    table = items.reshape(top, rows).T
    table = table[jax.random.permutation(jax.random.fold_in(own, 1), rows)]
    turn = jax.random.randint(jax.random.fold_in(own, 2), (rows, 1), 0, top)
    return jnp.take_along_axis(table, (jnp.arange(top)[None, :] + turn) % top, axis=1)


def portions_of(number_of, total, most, skew, full):
    portions = [(1 << 20) // math.isqrt(standing ** skew) + 1 for standing in range(1, number_of + 1)]
    largest = most if full else min(most, max(-(-total // number_of), total * portions[0] // sum(portions)))
    least = 1 if total - largest >= number_of - 1 else 0
    holding, surplus = [largest] + [least] * (number_of - 1), total - largest - least * (number_of - 1)
    while surplus > 0:
        free = [i for i in range(1, number_of) if holding[i] < largest] or [i for i in range(1, number_of) if holding[i] < most]
        mass, remaining = sum([portions[i] for i in free]), surplus
        for i in free:
            addition = min(most - holding[i], max(1, remaining * portions[i] // mass), surplus)
            holding[i] = holding[i] + addition
            surplus = surplus - addition
    return np.array(holding)


def normal_values(stream_key, extent, deviation, limit, pieces=(), dtype=jnp.bfloat16):
    loudness = steps_of(stream_key, extent, pieces, -0.22, 0.18) if pieces else 1.0
    values = jax.random.normal(stream_key, extent, jnp.float32) * deviation * loudness
    return jnp.minimum(jnp.maximum(values, -limit), limit).astype(dtype)


def setup_inputs(seed: int = 0) -> dict:
    key_list = jax.random.split(jax.random.key(seed), 8)
    visibilities = normal_values(key_list[0], (TILES, 2, TILE), 1.0, 6.0, ((0, 32),))
    positions = jnp.clip(1.0 * jax.random.uniform(key_list[1], (TILES, 2, TILE), jnp.float32) ** steps_of(key_list[1], (TILES, 2, TILE), ((0, 32),), -0.2, 0.2), 0.0, 1.0).astype(jnp.bfloat16)
    tile_scale = jnp.clip(jnp.exp(math.log(3.0) - 2.306499 * jax.random.uniform(key_list[2], (TILES,), jnp.float32) ** steps_of(key_list[2], (TILES,), ((0, 32),), -0.2, 0.2)), 0.29882812, 3.0).astype(jnp.bfloat16)
    owner_keys = jax.random.split(jax.random.fold_in(key_list[3], 1), TILES // TD)
    owner_turns = jax.random.permutation(jax.random.fold_in(key_list[3], 3), TILES // TD)
    owner = jax.vmap(lambda own, number: shared_out(jax.random.fold_in(key_list[3], 2), own, number, TD, N_UV, 1, CAP, 2))(owner_keys, owner_turns).reshape((TILES, 1))
    block_id = plant(jax.random.randint(key_list[4], (TILES,), 0, NBLK), jax.random.fold_in(key_list[4], 1), 0, NBLK - 1).astype(jnp.int32)
    w_slot = plant(jax.random.randint(key_list[5], (TILES,), 0, LAY_DEV), jax.random.fold_in(key_list[5], 1), 0, LAY_DEV - 1).astype(jnp.int32)
    screen = jnp.clip(jax.random.uniform(key_list[6], (LAYERS, ROWS, WC), jnp.float32, -3.140625, 3.140625), -3.140625, 3.140625).astype(jnp.bfloat16)
    return {"visibilities": visibilities, "positions": positions, "tile_scale": tile_scale, "owner": owner, "block_id": block_id, "w_slot": w_slot, "screen": screen}


def kernel_blocks(samples, coords, scales):
    tile_count = samples.shape[0]
    row_at = coords[:, 0, :].astype(jnp.float32) * KR
    col_at = coords[:, 1, :].astype(jnp.float32) * KC
    row_axis = jnp.arange(KR).astype(jnp.float32)
    col_axis = jnp.arange(KC).astype(jnp.float32)
    row_kern = jnp.sinc(row_axis[None, :, None] - row_at[:, None, :])
    col_kern = jnp.sinc(col_axis[None, None, :] - col_at[:, :, None]).astype(jnp.bfloat16)
    weighted = (samples.astype(jnp.float32)[:, :, None, :] * row_kern[:, None, :, :] * scales.astype(jnp.float32)[:, None, None, None]).astype(jnp.bfloat16)
    weighted = lax.optimization_barrier(weighted)
    col_kern = lax.optimization_barrier(col_kern)
    weighted = weighted.reshape(tile_count, 2 * KR, TILE).astype(jnp.float32)
    blocks = jnp.einsum("nrv,nvc->nrc", weighted, col_kern.astype(jnp.float32), precision=lax.Precision.HIGHEST)
    return blocks.reshape(tile_count, 2, KR, KC)


def reference(visibilities, positions, tile_scale, owner, block_id, w_slot, screen):
    batches = N_UV * N_WA

    def per_device(array):
        return array.reshape((batches, TD) + array.shape[1:])

    phase_table = screen.reshape(LAYERS, N_UV * BLK_R, KR, BLK_C, KC)
    device_ids = jnp.arange(batches).astype(jnp.int32)
    scanned = (per_device(visibilities), per_device(positions), per_device(tile_scale), per_device(owner[:, 0]), per_device(block_id), per_device(w_slot), device_ids)

    def one_device(running, device_item):
        samples, coords, scales, owners, block_ids, layer_ids, device_id = device_item
        blocks = kernel_blocks(samples, coords, scales)
        layer_of = (device_id % N_WA) * LAY_DEV + layer_ids
        band_row = owners * BLK_R + block_ids // BLK_C
        band_col = block_ids % BLK_C
        phases = phase_table[layer_of, band_row, :, band_col, :].astype(jnp.float32)
        cosine = jnp.cos(phases)
        sine_vals = jnp.sin(phases)
        real_part = cosine * blocks[:, 0] - sine_vals * blocks[:, 1]
        imag_part = sine_vals * blocks[:, 0] + cosine * blocks[:, 1]
        target = (owners * NBLK + block_ids).astype(jnp.int32)
        running = running.at[target].add(jnp.stack([real_part, imag_part], axis=1))
        return running, None

    zero_grid = jnp.zeros((N_UV * NBLK, 2, KR, KC), jnp.float32)
    running, unused = lax.scan(one_device, zero_grid, scanned)
    running = running.reshape(N_UV * BLK_R, BLK_C, 2, KR, KC)
    return running.transpose(2, 0, 3, 1, 4).reshape(2, ROWS, WC)
```

```python
import functools
import math

import jax
import jax.numpy as jnp
from jax import lax
from jax.experimental import pallas as pl
from jax.experimental.pallas import tpu as pltpu
from jax.sharding import PartitionSpec as P

KC = 128
UNROLL = 4
META = 16


def exchange(n_uv, n_wa, send_ref, recv_ref, send_sem, recv_sem, own_sem):
    me_u, me_a = lax.axis_index("uv"), lax.axis_index("wa")
    total = n_uv * n_wa

    def target(i):
        k, j = i // n_uv, i % n_uv
        return k, lax.rem(me_u + j, n_uv), lax.rem(me_a + k, n_wa)

    barrier = pltpu.get_barrier_semaphore()

    @pl.loop(1, total)
    def _(i):
        k, u, b = target(i)
        pl.semaphore_signal(barrier, inc=1, device_id=(u, b), device_id_type=pl.DeviceIdType.MESH)

    pl.semaphore_wait(barrier, total - 1)
    own = pltpu.make_async_copy(send_ref.at[me_u], recv_ref.at[me_u], own_sem)
    own.start()

    @pl.loop(1, total)
    def _(i):
        k, u, b = target(i)
        pltpu.make_async_remote_copy(
            src_ref=send_ref.at[k * n_uv + u],
            dst_ref=recv_ref.at[k * n_uv + me_u],
            send_sem=send_sem.at[k * n_uv + u],
            recv_sem=recv_sem.at[k * n_uv + me_u],
            device_id=(u, b),
            device_id_type=pl.DeviceIdType.MESH,
        ).start()

    own.wait()

    @pl.loop(1, total)
    def _(i):
        k, u, b = target(i)
        copy = pltpu.make_async_remote_copy(
            src_ref=send_ref.at[k * n_uv + u],
            dst_ref=recv_ref.at[k * n_uv + u],
            send_sem=send_sem.at[k * n_uv + u],
            recv_sem=recv_sem.at[k * n_uv + u],
            device_id=(u, b),
            device_id_type=pl.DeviceIdType.MESH,
        )
        copy.wait_send()
        copy.wait_recv()


def sin_pi_over_pi(d):
    z = d * d
    acc = jnp.full_like(z, 0.0)
    for n in range(6, -1, -1):
        acc = acc * z + ((-1) ** n * math.pi ** (2 * n) / math.factorial(2 * n + 1))
    return d * acc


def cos_sin(x):
    h = x * 0.5
    z = h * h
    s = jnp.full_like(z, 0.0)
    c = jnp.full_like(z, 0.0)
    for n in range(7, -1, -1):
        s = s * z + ((-1) ** n / math.factorial(2 * n + 1))
        c = c * z + ((-1) ** n / math.factorial(2 * n))
    s = s * h
    return 1.0 - 2.0 * s * s, 2.0 * s * c


def sinc_part(y, top, at_zero):
    r = pl.reciprocal(y, approx=True)
    r = r * (2.0 - y * r)
    return jnp.where(y == 0.0, at_zero, top * r)


def grid_kernel(kr, cap, first, slot_ref, block_ref, layer_ref, scale_ref, recv_ref, screen_ref, *rest):
    if first:
        out_ref, wide_ref, order_ref = rest
        out_ref[...] = jnp.zeros_like(out_ref)
    else:
        prior_ref, out_ref, wide_ref, order_ref = rest
        out_ref[...] = prior_ref[...]
    sources, slots = recv_ref.shape[0], slot_ref.shape[0]

    @pl.loop(0, sources)
    def _(i):
        wide_ref[i] = recv_ref[i, : cap * 8, :].astype(jnp.float32)

    def place(i, count):
        order_ref[count] = i
        return count + slot_ref[i]

    count = lax.fori_loop(0, slots, place, 0)
    for i in range(UNROLL):
        order_ref[count + i] = 0

    row_at = lax.broadcasted_iota(jnp.int32, (kr, KC), 0).astype(jnp.float32)
    col_at = lax.broadcasted_iota(jnp.int32, (KC, KC), 0).astype(jnp.float32)
    row8 = lax.broadcasted_iota(jnp.int32, (8, KC), 0)
    unit = jnp.where(row8 < 6, float(kr), float(KC))
    odd = (lax.broadcasted_iota(jnp.int32, (kr, KC), 0) + lax.broadcasted_iota(jnp.int32, (kr, KC), 1)) % 2
    sign = (1 - 2 * odd).astype(jnp.float32)

    def one(step):
        slot = order_ref[step]
        scale = jnp.where(step < count, scale_ref[slot], 0.0)
        rows = wide_ref[slot // cap, pl.ds(pl.multiple_of((slot % cap) * 8, 8), 8), :]
        place = rows * unit
        near = jnp.floor(place + 0.5)
        parity = near - 2.0 * jnp.floor(near * 0.5)
        flip = 1.0 - 2.0 * parity
        top = sin_pi_over_pi(place - near) * flip
        vis = rows * scale
        parts, cols = [], []
        for h in range(2):
            kx = sinc_part(place[4 + h : 5 + h] - row_at, top[4 + h : 5 + h], flip[4 + h : 5 + h])
            parts.append(
                jnp.concatenate([kx * vis[h : h + 1], kx * vis[2 + h : 3 + h]], axis=0).astype(jnp.bfloat16)
            )
            cols.append(
                sinc_part(place[6 + h : 7 + h] - col_at, top[6 + h : 7 + h], flip[6 + h : 7 + h]).astype(jnp.bfloat16)
            )
        weighted = jnp.concatenate(parts, axis=1)
        kernel = jnp.concatenate(cols, axis=1)
        block = lax.dot_general(
            weighted, kernel, (((1,), (1,)), ((), ())), preferred_element_type=jnp.float32
        )
        where = pl.ds(pl.multiple_of(block_ref[slot] * KC, KC), KC)
        cosine, sine = cos_sin(screen_ref[layer_ref[slot], :, where].astype(jnp.float32))
        cosine, sine = cosine * sign, sine * sign
        real, imag = block[:kr], block[kr:]
        return where, cosine * real - sine * imag, sine * real + cosine * imag

    @pl.loop(0, (count + UNROLL - 1) // UNROLL)
    def _(group):
        done = [one(group * UNROLL + i) for i in range(UNROLL)]
        for where, real, imag in done:
            out_ref[0, :, where] += real
            out_ref[1, :, where] += imag


def shards(visibilities, positions, tile_scale, owner, block_id, w_slot, screen):
    n_uv, n_wa = lax.axis_size("uv"), lax.axis_size("wa")
    me_a = lax.axis_index("wa")
    tiles, _, samples = visibilities.shape
    layers, kr, width = screen.shape
    part = width // n_wa
    blocks = part // KC
    cap = max(2, 3 * tiles // (2 * n_uv))
    total = n_uv * n_wa

    pieces = []
    for k in range(n_wa):
        piece = lax.dynamic_slice_in_dim(screen, lax.rem(me_a + k, n_wa) * part, part, 2)
        if k:
            piece = lax.ppermute(piece, "wa", [(i, (i + k) % n_wa) for i in range(n_wa)])
        pieces.append(piece)

    target = lax.rem(block_id // blocks - me_a + n_wa, n_wa) * n_uv + owner[:, 0]
    same = (target[:, None] == target[None, :]) & (
        jnp.arange(tiles)[None, :] < jnp.arange(tiles)[:, None]
    )
    slot = target * cap + jnp.sum(same.astype(jnp.int32), axis=1)
    chosen = (jnp.arange(total * cap)[:, None] == slot[None, :]).astype(jnp.bfloat16)
    data = jnp.concatenate([visibilities, positions], axis=1).reshape(tiles, 4 * samples)
    sent = jnp.dot(chosen, data, preferred_element_type=jnp.float32).astype(jnp.bfloat16)
    facts = jnp.stack(
        [
            tile_scale,
            lax.rem(block_id, blocks).astype(jnp.bfloat16),
            w_slot.astype(jnp.bfloat16),
            jnp.ones((tiles,), jnp.bfloat16),
        ],
        axis=1,
    )
    facts = jnp.dot(chosen, facts, preferred_element_type=jnp.float32).astype(jnp.bfloat16)
    facts = facts.reshape(total, cap, 4).transpose(0, 2, 1)
    facts = jnp.pad(facts, ((0, 0), (0, META - 4), (0, KC - cap)))
    send = jnp.concatenate([sent.reshape(total, cap * 8, KC), facts], axis=1)

    rows = cap * 8 + META
    recv = pl.pallas_call(
        functools.partial(exchange, n_uv, n_wa),
        out_shape=jax.ShapeDtypeStruct((total, rows, KC), jnp.bfloat16),
        in_specs=[pl.BlockSpec(memory_space=pl.ANY)],
        out_specs=pl.BlockSpec(memory_space=pl.ANY),
        scratch_shapes=[
            pltpu.SemaphoreType.DMA((total,)),
            pltpu.SemaphoreType.DMA((total,)),
            pltpu.SemaphoreType.DMA,
        ],
        compiler_params=pltpu.CompilerParams(collective_id=0, has_side_effects=True),
        cost_estimate=pl.CostEstimate(flops=0, bytes_accessed=total * rows * KC * 4, transcendentals=0),
        name="exchange",
    )(send)

    got = recv[:, cap * 8 : cap * 8 + 4, :cap].astype(jnp.float32)
    scales = got[:, 0].reshape(n_wa, n_uv * cap)
    ints = got[:, 1:].astype(jnp.int32)
    merged = None
    for k in range(n_wa):
        first = k == 0
        slots = n_uv * cap
        here = ints[k * n_uv : (k + 1) * n_uv]
        smem = pl.BlockSpec(memory_space=pltpu.SMEM)
        vmem = pl.BlockSpec(memory_space=pltpu.VMEM)
        merged = pl.pallas_call(
            functools.partial(grid_kernel, kr, cap, first),
            out_shape=jax.ShapeDtypeStruct((2, kr, part), jnp.float32),
            grid=(1,),
            in_specs=[
                smem,
                smem,
                smem,
                smem,
                pl.BlockSpec((n_uv, rows, KC), functools.partial(lambda at, i: (at, 0, 0), k)),
                vmem,
            ]
            + ([] if first else [vmem]),
            out_specs=vmem,
            scratch_shapes=[
                pltpu.VMEM((n_uv, cap * 8, KC), jnp.float32),
                pltpu.SMEM((slots + UNROLL,), jnp.int32),
            ],
            compiler_params=pltpu.CompilerParams(vmem_limit_bytes=48 * 2**20),
            cost_estimate=pl.CostEstimate(
                flops=2 * slots * 2 * kr * samples * KC, bytes_accessed=8 * 2**20, transcendentals=0
            ),
            name="grid_first" if first else "grid_next",
        )(
            here[:, 2].reshape(slots),
            here[:, 0].reshape(slots),
            here[:, 1].reshape(slots),
            scales[k],
            recv,
            pieces[k],
            *([] if first else [merged]),
        )
    return merged


def solution(mesh):
    return jax.shard_map(
        shards,
        mesh=mesh,
        in_specs=(
            P(("uv", "wa"), None, None),
            P(("uv", "wa"), None, None),
            P(("uv", "wa")),
            P(("uv", "wa"), None),
            P(("uv", "wa")),
            P(("uv", "wa")),
            P("wa", "uv", None),
        ),
        out_specs=P(None, "uv", "wa"),
        check_vma=False,
    )
```

```python
import functools
import math

import jax
import jax.numpy as jnp
from jax import lax
from jax.experimental import pallas as pl
from jax.experimental.pallas import tpu as pltpu
from jax.sharding import PartitionSpec as P

KC = 128
UNROLL = 4
META = 16


def exchange(n_uv, send_ref, recv_ref, send_sem, recv_sem, own_sem):
    me_u, me_a = lax.axis_index("uv"), lax.axis_index("wa")
    barrier = pltpu.get_barrier_semaphore()

    @pl.loop(1, n_uv)
    def _(j):
        u = lax.rem(me_u + j, n_uv)
        pl.semaphore_signal(barrier, inc=1, device_id=(u, me_a), device_id_type=pl.DeviceIdType.MESH)

    own = pltpu.make_async_copy(send_ref.at[me_u], recv_ref.at[me_u], own_sem)
    own.start()
    pl.semaphore_wait(barrier, n_uv - 1)

    @pl.loop(1, n_uv)
    def _(j):
        u = lax.rem(me_u + j, n_uv)
        pltpu.make_async_remote_copy(
            src_ref=send_ref.at[u],
            dst_ref=recv_ref.at[me_u],
            send_sem=send_sem.at[u],
            recv_sem=recv_sem.at[me_u],
            device_id=(u, me_a),
            device_id_type=pl.DeviceIdType.MESH,
        ).start()

    own.wait()

    @pl.loop(1, n_uv)
    def _(j):
        u = lax.rem(me_u + j, n_uv)
        copy = pltpu.make_async_remote_copy(
            src_ref=send_ref.at[u],
            dst_ref=recv_ref.at[u],
            send_sem=send_sem.at[u],
            recv_sem=recv_sem.at[u],
            device_id=(u, me_a),
            device_id_type=pl.DeviceIdType.MESH,
        )
        copy.wait_send()
        copy.wait_recv()


def patch_kernel(width, code_ref, screen_ref, out_ref):
    blocks = width // KC
    slots = out_ref.shape[0]

    @pl.loop(0, slots // 2)
    def _(pair):
        for i in range(2):
            slot = pair * 2 + i
            code = code_ref[slot]
            where = pl.ds(pl.multiple_of(lax.rem(code, blocks) * KC, KC), KC)
            layer = jnp.maximum(lax.div(code, blocks) - 1, 0)
            layer = lax.rem(layer, screen_ref.shape[0])
            out_ref[slot] = screen_ref[layer, :, where]


def sin_pi_over_pi(d):
    z = d * d
    acc = jnp.full_like(z, 0.0)
    for n in range(6, -1, -1):
        acc = acc * z + ((-1) ** n * math.pi ** (2 * n) / math.factorial(2 * n + 1))
    return d * acc


def cos_sin(x):
    h = x * 0.5
    z = h * h
    s = jnp.full_like(z, 0.0)
    c = jnp.full_like(z, 0.0)
    for n in range(7, -1, -1):
        s = s * z + ((-1) ** n / math.factorial(2 * n + 1))
        c = c * z + ((-1) ** n / math.factorial(2 * n))
    s = s * h
    return 1.0 - 2.0 * s * s, 2.0 * s * c


def sinc_part(y, top, at_zero):
    r = pl.reciprocal(y, approx=True)
    r = r * (2.0 - y * r)
    return jnp.where(y == 0.0, at_zero, top * r)


def grid_kernel(kr, cap, first, code_ref, scale_ref, recv_ref, patch_ref, *rest):
    if first:
        out_ref, wide_ref, order_ref = rest
        out_ref[...] = jnp.zeros_like(out_ref)
    else:
        prior_ref, out_ref, wide_ref, order_ref = rest
        out_ref[...] = prior_ref[...]
    sources, slots = recv_ref.shape[0], code_ref.shape[0]

    @pl.loop(0, sources)
    def _(i):
        wide_ref[i] = recv_ref[i, : cap * 8, :].astype(jnp.float32)

    def place(i, count):
        order_ref[count] = i
        return count + jnp.where(code_ref[i] >= 0, 1, 0)

    count = lax.fori_loop(0, slots, place, 0)
    for i in range(UNROLL):
        order_ref[count + i] = 0

    row_at = lax.broadcasted_iota(jnp.int32, (kr, KC), 0).astype(jnp.float32)
    col_at = lax.broadcasted_iota(jnp.int32, (KC, KC), 0).astype(jnp.float32)
    row8 = lax.broadcasted_iota(jnp.int32, (8, KC), 0)
    unit = jnp.where(row8 < 6, float(kr), float(KC))
    odd = (lax.broadcasted_iota(jnp.int32, (kr, KC), 0) + lax.broadcasted_iota(jnp.int32, (kr, KC), 1)) % 2
    sign = (1 - 2 * odd).astype(jnp.float32)

    def one(step):
        slot = order_ref[step]
        scale = jnp.where(step < count, scale_ref[slot], 0.0)
        rows = wide_ref[slot // cap, pl.ds(pl.multiple_of((slot % cap) * 8, 8), 8), :]
        place = rows * unit
        near = jnp.floor(place + 0.5)
        parity = near - 2.0 * jnp.floor(near * 0.5)
        flip = 1.0 - 2.0 * parity
        top = sin_pi_over_pi(place - near) * flip
        vis = rows * scale
        parts, cols = [], []
        for h in range(2):
            kx = sinc_part(place[4 + h : 5 + h] - row_at, top[4 + h : 5 + h], flip[4 + h : 5 + h])
            parts.append(
                jnp.concatenate([kx * vis[h : h + 1], kx * vis[2 + h : 3 + h]], axis=0).astype(jnp.bfloat16)
            )
            cols.append(
                sinc_part(place[6 + h : 7 + h] - col_at, top[6 + h : 7 + h], flip[6 + h : 7 + h]).astype(jnp.bfloat16)
            )
        weighted = jnp.concatenate(parts, axis=1)
        kernel = jnp.concatenate(cols, axis=1)
        block = lax.dot_general(
            weighted, kernel, (((1,), (1,)), ((), ())), preferred_element_type=jnp.float32
        )
        where = pl.ds(pl.multiple_of(jnp.maximum(code_ref[slot], 0) * KC, KC), KC)
        cosine, sine = cos_sin(patch_ref[slot].astype(jnp.float32))
        cosine, sine = cosine * sign, sine * sign
        real, imag = block[:kr], block[kr:]
        return where, cosine * real - sine * imag, sine * real + cosine * imag

    @pl.loop(0, (count + UNROLL - 1) // UNROLL)
    def _(group):
        done = [one(group * UNROLL + i) for i in range(UNROLL)]
        for where, real, imag in done:
            out_ref[0, :, where] += real
            out_ref[1, :, where] += imag


def shards(visibilities, positions, tile_scale, owner, block_id, w_slot, screen):
    n_uv, n_wa = lax.axis_size("uv"), lax.axis_size("wa")
    me_a = lax.axis_index("wa")
    tiles, _, samples = visibilities.shape
    layers, kr, width = screen.shape
    part = width // n_wa
    blocks = part // KC
    cap = max(2, 3 * tiles // (2 * n_uv))
    slots = n_uv * cap

    target = owner[:, 0]
    same = (target[:, None] == target[None, :]) & (
        jnp.arange(tiles)[None, :] < jnp.arange(tiles)[:, None]
    )
    slot = target * cap + jnp.sum(same.astype(jnp.int32), axis=1)
    chosen = (jnp.arange(slots)[:, None] == slot[None, :]).astype(jnp.bfloat16)
    data = jnp.concatenate([visibilities, positions], axis=1).reshape(tiles, 4 * samples)
    sent = jnp.dot(chosen, data, preferred_element_type=jnp.float32).astype(jnp.bfloat16)
    facts = jnp.stack(
        [
            tile_scale,
            lax.rem(block_id, blocks).astype(jnp.bfloat16),
            lax.div(block_id, blocks).astype(jnp.bfloat16),
            (w_slot + 1).astype(jnp.bfloat16),
        ],
        axis=1,
    )
    facts = jnp.dot(chosen, facts, preferred_element_type=jnp.float32).astype(jnp.bfloat16)
    facts = facts.reshape(n_uv, cap, 4).transpose(0, 2, 1)
    facts = jnp.pad(facts, ((0, 0), (0, META - 4), (0, KC - cap)))
    send = jnp.concatenate([sent.reshape(n_uv, cap * 8, KC), facts], axis=1)

    rows = cap * 8 + META
    smem = pl.BlockSpec(memory_space=pltpu.SMEM)
    vmem = pl.BlockSpec(memory_space=pltpu.VMEM)
    arrived = pl.pallas_call(
        functools.partial(exchange, n_uv),
        out_shape=jax.ShapeDtypeStruct((n_uv, rows, KC), jnp.bfloat16),
        in_specs=[pl.BlockSpec(memory_space=pl.ANY)],
        out_specs=pl.BlockSpec(memory_space=pl.ANY),
        scratch_shapes=[
            pltpu.SemaphoreType.DMA((n_uv,)),
            pltpu.SemaphoreType.DMA((n_uv,)),
            pltpu.SemaphoreType.DMA,
        ],
        compiler_params=pltpu.CompilerParams(collective_id=0, has_side_effects=True),
        cost_estimate=pl.CostEstimate(flops=0, bytes_accessed=n_uv * rows * KC * 4, transcendentals=0),
        name="exchange",
    )(send)

    def scalars(recv):
        got = recv[:, cap * 8 : cap * 8 + 4, :cap].astype(jnp.float32)
        ints = got[:, 1:].astype(jnp.int32).transpose(1, 0, 2).reshape(3, slots)
        return got[:, 0].reshape(slots), ints[0], ints[1], ints[2]

    facts_own = scalars(arrived)
    code = (facts_own[3] * n_wa + facts_own[2]) * blocks + facts_own[1]
    patches = pl.pallas_call(
        functools.partial(patch_kernel, width),
        out_shape=jax.ShapeDtypeStruct((slots, kr, KC), jnp.bfloat16),
        in_specs=[smem, vmem],
        out_specs=vmem,
        compiler_params=pltpu.CompilerParams(vmem_limit_bytes=32 * 2**20),
        cost_estimate=pl.CostEstimate(flops=0, bytes_accessed=3 * 2**20, transcendentals=0),
        name="patches",
    )(code, screen)

    merged = None
    for k in range(n_wa):
        first = k == 0
        recv, patch = arrived, patches
        if k:
            turn = [(i, (i + k) % n_wa) for i in range(n_wa)]
            recv, patch = lax.ppermute(recv, "wa", turn), lax.ppermute(patch, "wa", turn)
        scale, local, part_at, layer = scalars(recv) if k else facts_own
        here = jnp.where((layer > 0) & (part_at == me_a), local, -1)
        merged = pl.pallas_call(
            functools.partial(grid_kernel, kr, cap, first),
            out_shape=jax.ShapeDtypeStruct((2, kr, part), jnp.float32),
            in_specs=[smem, smem, vmem, vmem] + ([] if first else [vmem]),
            out_specs=vmem,
            scratch_shapes=[
                pltpu.VMEM((n_uv, cap * 8, KC), jnp.float32),
                pltpu.SMEM((slots + UNROLL,), jnp.int32),
            ],
            compiler_params=pltpu.CompilerParams(vmem_limit_bytes=32 * 2**20),
            cost_estimate=pl.CostEstimate(
                flops=2 * slots * 2 * kr * samples * KC, bytes_accessed=16 * 2**20, transcendentals=0
            ),
            name="grid_first" if first else "grid_next",
        )(here, scale, recv, patch, *([] if first else [merged]))
    return merged


def solution(mesh):
    return jax.shard_map(
        shards,
        mesh=mesh,
        in_specs=(
            P(("uv", "wa"), None, None),
            P(("uv", "wa"), None, None),
            P(("uv", "wa")),
            P(("uv", "wa"), None),
            P(("uv", "wa")),
            P(("uv", "wa")),
            P("wa", "uv", None),
        ),
        out_specs=P(None, "uv", "wa"),
        check_vma=False,
    )
```
